512 devices in a mesh: tp: 32 (over z, y_hi), ep: 16 (over y_lo, x, core).
Axes of the slice: x: 4, y: 8 (y_hi: 4, y_lo: 2; y = y_hi * 2 + y_lo), z: 8, core: 2. Of those that a mesh axis runs over, the one named last changes fastest.
Arguments:
- tokens: bfloat16 [16, 96, 7168], P('ep', 'tp'), may hold values from -6 to 6
- gain: float32 [7168], replicated, may hold values from 0.25 to 1.75
- routes: int32 [16, 96, 2], P('ep', 'tp'), may hold values from 0 to 15, all different within a row; in each aligned block of 96 rows (0 to 95, 96 to 191, ..., all dimensions but the last counted through in order) at most 18 rows name the same one
- gate_frac: int32 [16, 96, 2], P('ep', 'tp'), may hold values from 1 to 255
- dense_gate: bfloat16 [7168, 4864], P('ep', 'tp'), may hold values from -0.0625 to 0.0625
- dense_up: bfloat16 [7168, 4864], P('ep', 'tp'), may hold values from -0.0625 to 0.0625
- dense_down: bfloat16 [4864, 7168], P('tp', 'ep'), may hold values from -0.15625 to 0.15625
- expert_gate: bfloat16 [16, 7168, 2432], P('ep', 'tp'), may hold values from -0.0625 to 0.0625
- expert_up: bfloat16 [16, 7168, 2432], P('ep', 'tp'), may hold values from -0.0625 to 0.0625
- expert_down: bfloat16 [16, 2432, 7168], P('ep', None, 'tp'), may hold values from -0.125 to 0.125
Outputs:
- mixed: bfloat16 [16, 96, 7168], P('ep', None, 'tp')
The draws below stay inside these ranges and needn't reach their ends.
Inputs may be any that keep to these rules, and one draw needn't show every extreme that they name: `routes`: the two experts of a token differ. Among the 96 tokens of one index of the first dimension no expert is named more than 18 times, and in every draw some expert is named exactly 18 times by some such group. A route's weight is gate_frac / 256.
All inputs are finite; a program needn't handle non-finite values.
Results may differ from the reference program's by a relative error of at most 0.033.
Values may be sent and summed in bfloat16 or wider, within the bound.
No kernel may reach another device: no remote copies, remote signals or barrier semaphores. Data moves between devices by JAX's collectives and lax.ppermute only.
A program may use at most 64 MiB of HBM per device.

```python
import math
import jax
import jax.numpy as jnp
import numpy as np
from jax import lax

D = 7168
FF = 4864
EFF = 2432
RG = 96
TOKENS = 1536
EXPERTS = 16
CAP = 18
N_TP = 32
N_EP = 16


def touch_ends(array, key, low, top_value):
    extent = array.shape
    spot = [jax.random.randint(jax.random.fold_in(key, axis), (), 0, extent[axis]) for axis in range(len(extent))]
    array = array.at[tuple(spot)].set(low)
    longest = extent.index(max(extent))
    spot[longest] = (spot[longest] + 1) % extent[longest]
    return array.at[tuple(spot)].set(top_value)


def strengthened(values, key, source, target, blocks, factor):
    owner, partner = [(jnp.arange(values.shape[dim]) // (values.shape[dim] // blocks)).reshape([-1 if axis == dim else 1 for axis in range(values.ndim)]) for dim in (source, target)]
    chosen = jax.random.permutation(key, blocks)[partner]
    strong = (owner == chosen) | (owner == (partner + blocks // 2) % blocks)
    return jnp.where(strong, factor * values, values)


def block_levels(stream_key, extent, shards, low, top_value):
    factor_of = 1.0
    for axis_at, shards_of in shards:
        draws = jax.random.uniform(jax.random.fold_in(jax.random.fold_in(stream_key, 6), axis_at), (shards_of,), jnp.float32, low / len(shards), top_value / len(shards))
        factor_of = factor_of * jnp.repeat(jnp.exp(draws), extent[axis_at] // shards_of).reshape((-1,) + (1,) * (len(extent) - 1 - axis_at))
    return factor_of


def assign_block(key, own, number, rows, amount, top, limit, skew):
    sequence = jax.random.permutation(key, amount)
    heavy_load, ordinary = load_shares(amount, rows * top, limit, skew, True), load_shares(amount, rows * top, limit, skew, False)
    places = jnp.arange(amount)

    def named(lengths, turn):
        used = int((lengths > 0).sum())
        fixed = max(1, used // 4)
        moved = fixed + (places - fixed + turn * (used - fixed)) % max(1, amount - fixed)
        return jnp.zeros((amount,), jnp.int32).at[sequence[jnp.where(places < fixed, places, moved)]].set(jnp.asarray(lengths, jnp.int32))

    lengths = jnp.where(number % 4 == 0, named(heavy_load, number // 4), named(ordinary, number - number // 4 - 1))
    mixed = jax.random.permutation(jax.random.fold_in(own, 3), amount)
    donor, taker = mixed[0:amount // 2 * 2:2], mixed[1:amount // 2 * 2:2]
    room = jnp.minimum(lengths[donor] - 1, limit - lengths[taker]) // 2
    room = jnp.where((donor == sequence[0]) | (taker == sequence[0]) | (lengths[taker] == 0), 0, jnp.maximum(room, 0))
    moved = jax.random.randint(jax.random.fold_in(own, 4), (amount // 2,), 0, 1 << 20) % (room + 1)
    lengths = lengths.at[donor].add(-moved).at[taker].add(moved)
    members = jnp.searchsorted(jnp.cumsum(lengths), jnp.arange(rows * top), side="right").astype(jnp.int32)
    grid = members.reshape(top, rows).T
    grid = grid[jax.random.permutation(jax.random.fold_in(own, 1), rows)]
    turn = jax.random.randint(jax.random.fold_in(own, 2), (rows, 1), 0, top)
    return jnp.take_along_axis(grid, (jnp.arange(top)[None, :] + turn) % top, axis=1)


def load_shares(number_of, total, most, lean, full):
    loads = [(1 << 20) // math.isqrt(standing ** lean) + 1 for standing in range(1, number_of + 1)]
    largest = most if full else min(most, max(-(-total // number_of), total * loads[0] // sum(loads)))
    least = 1 if total - largest >= number_of - 1 else 0
    holding, rest = [largest] + [least] * (number_of - 1), total - largest - least * (number_of - 1)
    while rest > 0:
        free = [i for i in range(1, number_of) if holding[i] < largest] or [i for i in range(1, number_of) if holding[i] < most]
        whole, left = sum([loads[i] for i in free]), rest
        for i in free:
            more = min(most - holding[i], max(1, left * loads[i] // whole), rest)
            holding[i] = holding[i] + more
            rest = rest - more
    return np.array(holding)


def gaussian(stream_key, dims, width, bound, split=(), kind=jnp.bfloat16):
    level = block_levels(stream_key, dims, split, -0.22, 0.18) if split else 1.0
    values = jax.random.normal(stream_key, dims, jnp.float32) * width * level
    return jnp.minimum(jnp.maximum(values, -bound), bound).astype(kind)


def noise_with(rng, extent, scale, limit, cuts, heavy, kind=jnp.bfloat16):
    values = scale * jax.random.normal(rng, extent, jnp.float32)
    if cuts:
        values = values * block_levels(rng, extent, cuts, -0.22, 0.18)
    return jnp.clip(strengthened(values, jax.random.fold_in(rng, 3), *heavy), -limit, limit).astype(kind)


def setup_inputs(seed: int = 0) -> dict:
    arg_keys = jax.random.split(jax.random.key(seed), 11)
    tokens = gaussian(arg_keys[0], (N_EP, RG, D), 1.0, 6.0, ((0, 16), (1, 32)))
    gain = jnp.clip(1.0 + 0.15 * jax.random.normal(arg_keys[1], (D,), jnp.float32), 0.25, 1.75)
    routes_keys = jax.random.split(jax.random.fold_in(arg_keys[2], 1), N_EP * RG // RG)
    routes_turns = jax.random.permutation(jax.random.fold_in(arg_keys[2], 3), N_EP * RG // RG)
    routes = jax.vmap(lambda own, number: assign_block(jax.random.fold_in(arg_keys[2], 2), own, number, RG, EXPERTS, 2, CAP, 1))(routes_keys, routes_turns).reshape((N_EP, RG, 2))
    gate_frac = touch_ends(jax.random.randint(arg_keys[3], (N_EP, RG, 2), 1, 256), jax.random.fold_in(arg_keys[3], 1), 1, 255).astype(jnp.int32)
    dense_gate = gaussian(arg_keys[4], (D, FF), D ** -0.5, 0.0625, ((0, 16), (1, 32)))
    dense_up = gaussian(arg_keys[5], (D, FF), D ** -0.5, 0.0625, ((0, 16), (1, 32)))
    dense_down = noise_with(arg_keys[6], (FF, D), FF ** -0.5, 0.15625, ((0, 32), (1, 16)), (0, 1, 32, 2.75))
    expert_gate = gaussian(arg_keys[7], (EXPERTS, D, EFF), D ** -0.5, 0.0625, ((0, 16), (1, 32)))
    expert_up = gaussian(arg_keys[8], (EXPERTS, D, EFF), D ** -0.5, 0.0625, ((0, 16), (1, 32)))
    expert_down = gaussian(arg_keys[9], (EXPERTS, EFF, D), EFF ** -0.5, 0.125, ((0, 16), (2, 32)))
    return {"tokens": tokens, "gain": gain, "routes": routes, "gate_frac": gate_frac, "dense_gate": dense_gate, "dense_up": dense_up, "dense_down": dense_down, "expert_gate": expert_gate, "expert_up": expert_up, "expert_down": expert_down}


EPS = 1e-05

def rms_norm(rows, gain):
    values = rows.astype(jnp.float32)
    scale = lax.rsqrt(lax.optimization_barrier(jnp.mean(values * values, axis=-1, keepdims=True)) + EPS)
    return (values * scale * gain).astype(jnp.bfloat16)

def rounded_term(values):
    return lax.optimization_barrier(values.astype(jnp.bfloat16)).astype(jnp.float32)

def reference(tokens, gain, routes, gate_frac, dense_gate, dense_up, dense_down, expert_gate, expert_up, expert_down):
    flat_rows = tokens.reshape(TOKENS, D)
    normed = rms_norm(flat_rows, gain)
    gate_pre = jnp.dot(normed, dense_gate, preferred_element_type=jnp.float32)
    up_pre = jnp.dot(normed, dense_up, preferred_element_type=jnp.float32)
    dense_hidden = (jax.nn.silu(gate_pre) * up_pre).astype(jnp.bfloat16)
    block_width = FF // N_TP

    def dense_step(total, block):
        start = block * block_width
        hidden_part = lax.dynamic_slice_in_dim(dense_hidden, start, block_width, 1)
        weight_part = lax.dynamic_slice_in_dim(dense_down, start, block_width, 0)
        term = rounded_term(jnp.dot(hidden_part, weight_part, preferred_element_type=jnp.float32))
        return (total + term, None)
    dense_out, _ = lax.scan(dense_step, jnp.zeros((TOKENS, D), jnp.float32), jnp.arange(N_TP, dtype=jnp.int32))
    route_ids = routes.reshape(-1)
    route_weight = gate_frac.reshape(-1).astype(jnp.float32) / 256.0
    owner = jnp.arange(TOKENS * 2, dtype=jnp.int32) // 2
    most = N_EP * CAP
    slice_width = D // N_TP

    def expert_step(total, expert):
        chosen = route_ids == expert
        count = jnp.cumsum(chosen.astype(jnp.int32)) - 1
        target = jnp.where(chosen, count, most).astype(jnp.int32)
        source = jnp.zeros((most,), jnp.int32).at[target].set(owner, mode='drop')
        picked = normed[source]
        blocks = picked.reshape(most, N_TP, slice_width).astype(jnp.float32)
        gate_w = lax.dynamic_index_in_dim(expert_gate, expert, 0, keepdims=False).reshape(N_TP, slice_width, EFF).astype(jnp.float32)
        up_w = lax.dynamic_index_in_dim(expert_up, expert, 0, keepdims=False).reshape(N_TP, slice_width, EFF).astype(jnp.float32)
        gate_sum = lax.optimization_barrier(jnp.sum(rounded_term(jnp.einsum('rjd,jdh->rjh', blocks, gate_w)), axis=1))
        up_sum = lax.optimization_barrier(jnp.sum(rounded_term(jnp.einsum('rjd,jdh->rjh', blocks, up_w)), axis=1))
        hidden = (jax.nn.silu(gate_sum) * up_sum).astype(jnp.bfloat16)
        down_w = lax.dynamic_index_in_dim(expert_down, expert, 0, keepdims=False)
        result = rounded_term(jnp.dot(hidden, down_w, preferred_element_type=jnp.float32))
        slot = jnp.clip(count, 0, most - 1).reshape(TOKENS, 2)
        weight = jnp.where(chosen, route_weight, jnp.float32(0.0)).reshape(TOKENS, 2)
        total = total + result[slot[:, 0]] * weight[:, 0:1] + result[slot[:, 1]] * weight[:, 1:2]
        return (total, None)
    moe_out, _ = lax.scan(expert_step, jnp.zeros((TOKENS, D), jnp.float32), jnp.arange(EXPERTS, dtype=jnp.int32))
    return (dense_out + moe_out).astype(jnp.bfloat16).reshape(N_EP, RG, D)
```

```python
import jax
import jax.numpy as jnp
from jax import lax
from jax.sharding import PartitionSpec as P

D = 7168


EPS = 1e-05


def rms_norm(rows, gain):
    values = rows.astype(jnp.float32)
    scale = lax.rsqrt(jnp.mean(values * values, axis=-1, keepdims=True) + EPS)
    return (values * scale * gain).astype(jnp.bfloat16)


def swish_product(gate_pre, up_pre):
    return (jax.nn.silu(gate_pre) * up_pre).astype(jnp.bfloat16)


def share(block, axis):
    copies = jnp.broadcast_to(block[None], (lax.axis_size(axis), *block.shape))
    return lax.all_to_all(lax.optimization_barrier(copies), axis, 0, 0, tiled=True)


def exchange_sum(blocks, axis):
    moved = lax.all_to_all(blocks, axis, 0, 0, tiled=True)
    return jnp.sum(moved.astype(jnp.float32), axis=0)


def local(
    tokens,
    gain,
    routes,
    gate_frac,
    dense_gate,
    dense_up,
    dense_down,
    expert_gate,
    expert_up,
    expert_down,
):
    tp_count = lax.axis_size("tp")
    ep_count = lax.axis_size("ep")
    normed = rms_norm(tokens[0], gain)
    small = jnp.concatenate([routes[0], gate_frac[0]], axis=1).astype(jnp.bfloat16)
    row = jnp.concatenate([normed, jnp.pad(small, ((0, 0), (0, 124)))], axis=1)
    arrived_rows = share(row, "tp").reshape(-1, D + 128)
    gathered = arrived_rows[:, :D]
    route_ids = arrived_rows[:, D : D + 2].astype(jnp.int32)
    fractions = arrived_rows[:, D + 2 : D + 4].astype(jnp.int32)
    group_rows = gathered.shape[0]
    capacity = 3 * group_rows // ep_count
    slot_count = ep_count * capacity
    slice_width = D // tp_count
    flat_ids = route_ids.reshape(-1)
    expert_hot = (flat_ids[:, None] == jnp.arange(ep_count, dtype=jnp.int32)[None, :]).astype(
        jnp.int32
    )
    earlier = jnp.cumsum(expert_hot, axis=0) - expert_hot
    position = jnp.sum(earlier * expert_hot, axis=1)
    slot_index = flat_ids * capacity + position
    slot_hot = (slot_index[:, None] == jnp.arange(slot_count, dtype=jnp.int32)[None, :]).astype(
        jnp.float32
    )
    route_weight = fractions.reshape(-1).astype(jnp.float32) / 256.0
    dispatch_table = slot_hot.reshape(group_rows, 2, slot_count).sum(axis=1).astype(jnp.bfloat16)
    combine_table = (
        (slot_hot * route_weight[:, None])
        .reshape(group_rows, 2, slot_count)
        .sum(axis=1)
        .astype(jnp.bfloat16)
    )
    own_columns = lax.dynamic_slice_in_dim(
        gathered, lax.axis_index("tp") * slice_width, slice_width, 1
    )
    first = jnp.dot(
        gathered,
        lax.all_gather(dense_gate, "ep", axis=0, tiled=True),
        preferred_element_type=jnp.float32,
    )
    second = jnp.dot(
        gathered,
        lax.all_gather(dense_up, "ep", axis=0, tiled=True),
        preferred_element_type=jnp.float32,
    )
    dense_hidden = swish_product(first, second)
    partial_value = jnp.dot(
        dense_hidden,
        lax.all_gather(dense_down, "ep", axis=1, tiled=True),
        preferred_element_type=jnp.float32,
    ).astype(jnp.bfloat16)
    dense_out = exchange_sum(
        partial_value.reshape(group_rows, tp_count, slice_width).transpose(1, 0, 2), "tp"
    )
    outgoing = jnp.einsum(
        "rs,rd->sd", dispatch_table, own_columns, preferred_element_type=jnp.float32
    ).astype(jnp.bfloat16)
    arrived = lax.all_to_all(
        outgoing.reshape(ep_count, capacity, -1), "ep", split_axis=0, concat_axis=0, tiled=True
    ).reshape(slot_count, -1)
    terms = jnp.stack(
        [
            jnp.dot(arrived, expert_gate[0], preferred_element_type=jnp.float32),
            jnp.dot(arrived, expert_up[0], preferred_element_type=jnp.float32),
        ]
    ).astype(jnp.bfloat16)
    per_device = slot_count // tp_count
    gate_share, up_share = exchange_sum(
        terms.reshape(2, tp_count, per_device, -1).transpose(1, 0, 2, 3), "tp"
    )
    expert_hidden = share(swish_product(gate_share, up_share), "tp").reshape(slot_count, -1)
    expert_result = jnp.dot(
        expert_hidden, expert_down[0], preferred_element_type=jnp.float32
    ).astype(jnp.bfloat16)
    returned = lax.all_to_all(
        expert_result.reshape(ep_count, capacity, -1), "ep", split_axis=0, concat_axis=0, tiled=True
    ).reshape(slot_count, -1)
    moe_out = jnp.dot(combine_table, returned, preferred_element_type=jnp.float32)
    return (dense_out + moe_out).astype(jnp.bfloat16)[None]


def solution(mesh):
    placed = (
        P("ep", "tp", None),
        P(),
        P("ep", "tp", None),
        P("ep", "tp", None),
        P("ep", "tp"),
        P("ep", "tp"),
        P("tp", "ep"),
        P("ep", "tp", None),
        P("ep", "tp", None),
        P("ep", None, "tp"),
    )
    return jax.shard_map(
        local, mesh=mesh, in_specs=placed, out_specs=P("ep", None, "tp"), check_vma=False
    )
```

```python
import jax
import jax.numpy as jnp
import numpy as np
from jax import lax
from jax.experimental import pallas as pl
from jax.experimental.pallas import tpu as pltpu
from jax.sharding import Mesh, PartitionSpec as P

D = 7168
EPS = 1e-05
Z, YH, YL, X, C = 8, 4, 2, 4, 2
EP = YL * X * C
TP = Z * YH
ROWS = 96
CAP = 18
LAND = 24
SLOT = 20
EFF = 2432
HID = 640
FEAT = 224
HALF = 448
WIDE = 1024
BLOCK = 160
SHARE = 2 * BLOCK
MATES = 4
MOE_Z = EP * SLOT // Z
DENSE_Z = MATES * ROWS // Z // 2
ROW_Z = MOE_Z + DENSE_Z
BF, F32 = jnp.bfloat16, jnp.float32


def call(kernel, outs, args, scalars=(), scratch=(), flops=0):
    specs = [pl.BlockSpec(memory_space=pltpu.SMEM)] * len(scalars)
    specs += [pl.BlockSpec(memory_space=pltpu.VMEM)] * len(args)
    moved = sum(a.size * a.dtype.itemsize for a in args)
    moved += sum(o.size * o.dtype.itemsize for o in outs)
    single = len(outs) == 1
    return pl.pallas_call(
        kernel,
        out_shape=outs[0] if single else outs,
        in_specs=specs,
        out_specs=pl.BlockSpec(memory_space=pltpu.VMEM)
        if single
        else [pl.BlockSpec(memory_space=pltpu.VMEM)] * len(outs),
        scratch_shapes=list(scratch),
        compiler_params=pltpu.CompilerParams(vmem_limit_bytes=40 * 1024 * 1024),
        cost_estimate=pl.CostEstimate(flops=flops, bytes_accessed=moved, transcendentals=0),
    )(*scalars, *args)


def struct(shape, dtype=BF):
    return jax.ShapeDtypeStruct(shape, dtype)


def iota(shape, dim):
    return lax.broadcasted_iota(jnp.int32, shape, dim)


def dot(a, b):
    return jnp.dot(a, b, preferred_element_type=F32)


def rms_norm(rows, gain):
    values = rows.astype(F32)
    scale = lax.rsqrt(jnp.mean(values * values, axis=-1, keepdims=True) + EPS)
    return (values * scale * gain).astype(BF)


def dispatch_kernel(got, tokens_out, slots_out, mix_out):
    token, row = iota((ROWS, 4 * TP), 0), iota((ROWS, 4 * TP), 1)
    pick = (token == 3 * (row >> 2) + (row & 3)) & ((row & 3) < 3)
    tokens = dot(pick.astype(F32).astype(BF), got[...]).astype(BF)
    tokens_out[...] = tokens
    meta = jnp.transpose(tokens[:, 384:512].astype(F32), (1, 0))
    first, second = meta[64:65, :], meta[65:66, :]
    expert = iota((EP, ROWS), 0).astype(F32)
    hot_a = (expert == first).astype(F32)
    hot_b = (expert == second).astype(F32)
    earlier = (iota((ROWS, ROWS), 0) < iota((ROWS, ROWS), 1)).astype(F32).astype(BF)
    count = dot((hot_a + hot_b).astype(BF), earlier)
    slot_a = first * LAND + jnp.sum(hot_a * count, axis=0, keepdims=True)
    slot_b = second * LAND + jnp.sum(hot_b * count, axis=0, keepdims=True)
    slot = iota((EP * LAND, ROWS), 0).astype(F32)
    at_a, at_b = (slot == slot_a).astype(F32), (slot == slot_b).astype(F32)
    slots_out[...] = dot((at_a + at_b).astype(BF), tokens).astype(BF)
    mix = (at_a * meta[66:67, :] + at_b * meta[67:68, :]) * (1.0 / 256.0)
    mix_out[...] = jnp.transpose(mix, (1, 0)).astype(BF)


def assemble_kernel(me, part0, part1, part2, part3, gate_out, up_out):
    for out in (gate_out, up_out):
        for half in range(2):
            out[512 * half + HALF : 512 * (half + 1), :] = jnp.zeros((64, HID), BF)
    for k, part in enumerate((part0, part1, part2, part3)):
        source = me[0] ^ k
        start = pl.multiple_of((source >> 1) * 512 + (source & 1) * FEAT, 16)
        gate_out[pl.ds(start, FEAT), :] = part[0:FEAT, :]
        up_out[pl.ds(start, FEAT), :] = part[FEAT : 2 * FEAT, :]


def dense_up_kernel(column, mate, rows, weights, out, held):
    lane = iota((BLOCK, 128), 1)

    def put(branch, first, half, width, values):
        for low, high, place in ((0, 256, 256 * branch), (256, SHARE, 512 + 64 * branch)):
            begin, end = max(first, low), min(first + BLOCK, high)
            if begin < end:
                held[place + begin - low : place + end - low, half : half + width] = values[
                    begin - first : end - first, :
                ]

    for half in range(2):
        for q in range(2):
            part = weights.at[(2 * half + q) ^ column[0]]
            tail = part[:, 768:896].astype(F32)
            tails = (tail, pltpu.roll(tail, 64, 1))
            for branch in range(2):
                put(branch, q * BLOCK, 512 * half, 384, part[:, 384 * branch : 384 * (branch + 1)])
                last = jnp.where(lane < 64, tails[branch], 0.0).astype(BF)
                put(branch, q * BLOCK, 512 * half + 384, 128, last)
    for i in range(MATES):
        out[ROWS * i : ROWS * (i + 1), :] = lax.dot_general(
            rows[mate[0] ^ i], held[...], (((1,), (1,)), ((), ())), preferred_element_type=F32
        ).astype(BF)


def expert_up_kernel(got, gate, up, dense, out):
    row, column = iota((EP * SLOT, EP * LAND), 0), iota((EP * SLOT, EP * LAND), 1)
    group = ((row.astype(F32) + 0.5) * (1.0 / SLOT)).astype(jnp.int32)
    place = row - SLOT * group
    pick = (column == LAND * group + place) & (place < CAP)
    rows = dot(pick.astype(F32).astype(BF), got[...]).astype(BF)
    for branch, weights in enumerate((gate, up)):
        pre = dot(rows, weights[...])
        other = dense[...].astype(F32)
        for z in range(Z):
            out[z, :, HID * branch : HID * (branch + 1)] = jnp.concatenate(
                [
                    pre[MOE_Z * z : MOE_Z * (z + 1)],
                    other[DENSE_Z * (2 * z + branch) : DENSE_Z * (2 * z + branch + 1)],
                ],
                axis=0,
            ).astype(BF)


def swish(gate, up):
    return gate / (1.0 + jnp.exp(-gate)) * up


def hidden_kernel(me, got, out):
    total = got[0].astype(F32)
    for z in range(1, Z):
        total = total + got[z].astype(F32)
    expert = swish(total[:MOE_Z, :HID], total[:MOE_Z, HID:])
    twice = iota((MOE_Z, HID), 1) < YH * HID - EFF
    expert = jnp.where(twice & (me[0] == YH - 1), 0.0, expert)
    pieces, tails = [], []
    for half in range(2):
        rows = total[MOE_Z:, HID * half : HID * (half + 1)]
        pieces.append(swish(rows[:, :256], rows[:, 256:512]))
        tail = rows[:, 512:640]
        tails.append(swish(tail, pltpu.roll(tail, 64, 1)))
    lane = iota((DENSE_Z, 128), 1)
    pieces.append(jnp.where(lane < 64, tails[0], pltpu.roll(tails[1], 64, 1)))
    hidden = jnp.concatenate([expert, jnp.concatenate(pieces, axis=1)], axis=0).astype(BF)
    for z in range(Z):
        out[z] = hidden


def dense_down_kernel(column, got, dense, own_out, *outs_and_held):
    *others, held = outs_and_held
    held[...] = jnp.zeros(held.shape, BF)
    for half in range(2):
        for side in range(2):
            for q in range(2):
                values = dense.at[(2 * half + q) ^ column[0]]
                first, left = q * BLOCK, 896 + 256 * side
                for low, high, step, place in ((0, 256, 256, 0), (256, SHARE, 64, 512)):
                    begin, end = max(first, low), min(first + BLOCK, high)
                    if begin < end:
                        for i in range(2):
                            at = place + step * i
                            held[2 * half + side, i, at + begin - low : at + end - low, :] = values[
                                begin - first : end - first, left : left + FEAT
                            ]
    rows = got[...].astype(F32)
    rows = jnp.concatenate(
        [rows[ROW_Z * z + MOE_Z : ROW_Z * (z + 1)] for z in range(Z)], axis=0
    ).astype(BF)
    for target in range(YH):
        sums = [dot(rows, held[target, i]) for i in range(2)]
        for mate, out in enumerate((own_out, *others)):
            pieces = []
            for z in (2 * mate, 2 * mate + 1):
                pieces += [part[DENSE_Z * z : DENSE_Z * (z + 1)] for part in sums]
            out[target] = jnp.concatenate(pieces, axis=0).astype(out.dtype)


def expert_down_kernel(me, got, part0, part1, part2, part3, out):
    rows = got[...].astype(F32)
    rows = jnp.concatenate(
        [rows[ROW_Z * z : ROW_Z * z + MOE_Z] for z in range(Z)], axis=0
    ).astype(BF)
    for k, part in enumerate((part0, part1, part2, part3)):
        out[me[0] ^ k] = lax.dot_general(
            rows, part[...], (((1,), (1,)), ((), ())), preferred_element_type=F32
        ).astype(BF)


def result_kernel(got, slots_out, own_out):
    total = got[0].astype(F32)
    for k in range(1, YH):
        total = total + got[k].astype(F32)
    expert = total[: EP * SLOT]
    slot, row = iota((EP * LAND, EP * SLOT), 0), iota((EP * LAND, EP * SLOT), 1)
    group = ((slot.astype(F32) + 0.5) * (1.0 / LAND)).astype(jnp.int32)
    place = slot - LAND * group
    pick = (row == SLOT * group + place) & (place < CAP)
    slots_out[...] = dot(pick.astype(F32).astype(BF), expert.astype(BF)).astype(BF)
    own_out[...] = total[EP * SLOT :]


def turn_pairs():
    return [
        (z * EP + i, z * EP + ((i // C + z) % (YL * X)) * C + i % C)
        for z in range(Z)
        for i in range(EP)
    ]


def spread_pairs():
    pairs = []
    for z in range(Z):
        for i in range(EP):
            x, yl, c = (i % 2) * 2 + z % 2, z // 4, z // 2 % 2
            pairs.append((z * EP + i, (i // 2) * EP + yl * X * C + x * C + c))
    turned = dict(turn_pairs())
    return [(turned[source], target) for source, target in pairs]


SWAP = [(0, 1), (1, 0)]
CROSS = [(0, 3), (1, 2), (2, 1), (3, 0)]


def to_mates(first, second, third):
    return (
        lax.ppermute(first, "c", SWAP),
        lax.ppermute(second, "yl", SWAP),
        lax.ppermute(third, ("yl", "c"), CROSS),
    )


def local(
    tokens,
    gain,
    routes,
    gate_frac,
    dense_gate,
    dense_up,
    dense_down,
    expert_gate,
    expert_up,
    expert_down,
):
    position = lax.axis_index("yh")
    me = position.astype(jnp.int32).reshape(1)

    normed = rms_norm(tokens[0], gain)
    parts = jnp.pad(normed.reshape(3, Z, 2, HALF), ((0, 0), (0, 0), (0, 0), (0, 64)))
    small = jnp.concatenate([routes[0], gate_frac[0]], axis=1).astype(BF)
    small = jnp.pad(small, ((0, 0), (HALF, 60)))
    parts = parts + jnp.stack([small, jnp.zeros_like(small)], axis=1)[:, None]
    parts = jnp.pad(parts.reshape(3, Z, WIDE).transpose(1, 0, 2), ((0, 0), (0, 1), (0, 0)))
    send = jnp.broadcast_to(parts[:, None], (Z, YH, 4, WIDE)).reshape(TP, 4, WIDE)
    ups, downs = [], []
    for k in range(YH):
        start = HID * (position ^ k)
        ups.append(
            jnp.concatenate(
                [
                    lax.dynamic_slice_in_dim(expert_gate[0], start, HID, 1),
                    lax.dynamic_slice_in_dim(expert_up[0], start, HID, 1),
                ]
            )
        )
        downs.append(lax.dynamic_slice_in_dim(expert_down[0].T, start, HID, 1))

    def moved(block, k):
        return lax.ppermute(block, "yh", [(i, i ^ k) for i in range(YH)])

    for k in (1, 3):
        ups[k] = moved(ups[k], k)

    def padded(block):
        return jnp.pad(block, ((0, BLOCK - 152), (0, 0)))

    plane = ("z", "yl", "x", "c")
    gate_in, up_in, low = padded(dense_gate.T), padded(dense_up.T), padded(dense_down)
    dense = [gate_in[:, :384], up_in[:, :384], gate_in[:, 384:], up_in[:, 384:]]
    for side in range(2):
        part = low[:, FEAT * side : FEAT * (side + 1)]
        dense.append(jnp.pad(part, ((0, 0), (0, 256 - FEAT))))
    dense = lax.ppermute(jnp.concatenate(dense, axis=1), plane, turn_pairs())
    dense = lax.ppermute(dense, plane, spread_pairs())
    got = lax.all_to_all(send, ("z", "yh"), 0, 0, tiled=True).reshape(4 * TP, WIDE)
    column = lax.axis_index("x").astype(jnp.int32).reshape(1)
    own, slots, mix = call(
        dispatch_kernel,
        [struct((ROWS, WIDE)), struct((EP * LAND, WIDE)), struct((ROWS, EP * LAND))],
        [got],
        flops=2 * EP * LAND * ROWS * WIDE,
    )
    own, dense = lax.optimization_barrier((own, dense))
    mates = [lax.all_gather(own, ("yl", "c"), axis=0)]
    mate = (2 * lax.axis_index("yl") + lax.axis_index("c")).astype(jnp.int32).reshape(1)
    ups[2] = moved(ups[2], 2)
    dense = jnp.stack(
        [dense]
        + [lax.ppermute(dense, "x", [(i, i ^ k) for i in range(X)]) for k in range(1, X)]
    )
    arrived = lax.all_to_all(
        slots.reshape(EP, LAND, WIDE), ("yl", "x", "c"), 0, 0, tiled=True
    ).reshape(EP * LAND, WIDE)

    gate, up = call(
        assemble_kernel, [struct((WIDE, HID)), struct((WIDE, HID))], ups, scalars=[me]
    )
    gate, up, *mates = lax.optimization_barrier((gate, up, *mates))
    dense_pre = call(
        dense_up_kernel,
        [struct((MATES * ROWS, 2 * SHARE))],
        [*mates, dense],
        scalars=[column, mate],
        scratch=[pltpu.VMEM((2 * SHARE, WIDE), BF)],
        flops=4 * MATES * ROWS * WIDE * SHARE,
    )
    pre = call(
        expert_up_kernel,
        [struct((Z, ROW_Z, 2 * HID))],
        [arrived, gate, up, dense_pre],
        flops=4 * EP * SLOT * WIDE * HID,
    )
    pre, *downs = lax.optimization_barrier((pre, *downs))
    pre = lax.all_to_all(pre, "z", 0, 0, tiled=True)
    hidden = call(hidden_kernel, [struct((Z, ROW_Z, HID))], [pre], scalars=[me])
    downs[1:] = [moved(downs[k], k) for k in range(1, YH)]
    hidden, *downs = lax.optimization_barrier((hidden, *downs))
    hidden = lax.all_to_all(hidden, "z", 0, 0, tiled=True)
    hidden = hidden.reshape(Z * ROW_Z, HID)
    own_sum, *others = call(
        dense_down_kernel,
        [struct((YH, ROWS, FEAT), F32 if i == 0 else BF) for i in range(MATES)],
        [hidden, dense],
        scalars=[column],
        scratch=[pltpu.VMEM((YH, 2, HID, FEAT), BF)],
        flops=16 * MATES * ROWS * HID * FEAT,
    )
    from_mates = to_mates(*others)
    partial = call(
        expert_down_kernel,
        [struct((YH, EP * SLOT, FEAT))],
        [hidden, *downs],
        scalars=[me],
        flops=8 * EP * SLOT * HID * FEAT,
    )
    for sent in from_mates:
        own_sum = own_sum + sent.astype(F32)
    partial = jnp.concatenate([partial, own_sum.astype(BF)], axis=1)
    partial = lax.all_to_all(partial, "yh", 0, 0, tiled=True)
    result, own_sum = call(
        result_kernel,
        [struct((EP * LAND, FEAT)), struct((ROWS, FEAT), F32)],
        [partial],
        flops=2 * EP * LAND * EP * SLOT * FEAT,
    )
    returned = lax.all_to_all(
        result.reshape(EP, LAND, FEAT), ("yl", "x", "c"), 0, 0, tiled=True
    ).reshape(EP * LAND, FEAT)
    return (own_sum + dot(mix, returned)).astype(BF)[None]


def solution(mesh):
    split = Mesh(
        np.asarray(mesh.devices).reshape(Z, YH, YL, X, C), ("z", "yh", "yl", "x", "c")
    )
    tp, ep = ("z", "yh"), ("yl", "x", "c")
    placed = (
        P(ep, tp, None),
        P(),
        P(ep, tp, None),
        P(ep, tp, None),
        P(ep, tp),
        P(ep, tp),
        P(tp, ep),
        P(ep, tp, None),
        P(ep, tp, None),
        P(ep, None, tp),
    )
    return jax.shard_map(
        local, mesh=split, in_specs=placed, out_specs=P(ep, None, tp), check_vma=False
    )
```

```python
import jax
import jax.numpy as jnp
import numpy as np
from jax import lax
from jax.experimental import pallas as pl
from jax.experimental.pallas import tpu as pltpu
from jax.sharding import Mesh, PartitionSpec as P

D = 7168
EPS = 1e-05
Z, YH, YL, X, C = 8, 4, 2, 4, 2
EP = YL * X * C
TP = Z * YH
ROWS = 96
CAP = 18
LAND = 24
SLOT = 20
EFF = 2432
HID = 640
FEAT = 224
HALF = 448
WIDE = 1024
BLOCK = 160
SHARE = 2 * BLOCK
MATES = 4
MOE_Z = EP * SLOT // Z
DENSE_Z = MATES * ROWS // Z // 2
ROW_Z = MOE_Z + DENSE_Z
BF, F32 = jnp.bfloat16, jnp.float32


def call(kernel, outs, args, scalars=(), scratch=(), flops=0):
    specs = [pl.BlockSpec(memory_space=pltpu.SMEM)] * len(scalars)
    specs += [pl.BlockSpec(memory_space=pltpu.VMEM)] * len(args)
    moved = sum(a.size * a.dtype.itemsize for a in args)
    moved += sum(o.size * o.dtype.itemsize for o in outs)
    single = len(outs) == 1
    return pl.pallas_call(
        kernel,
        out_shape=outs[0] if single else outs,
        in_specs=specs,
        out_specs=pl.BlockSpec(memory_space=pltpu.VMEM)
        if single
        else [pl.BlockSpec(memory_space=pltpu.VMEM)] * len(outs),
        scratch_shapes=list(scratch),
        compiler_params=pltpu.CompilerParams(vmem_limit_bytes=40 * 1024 * 1024),
        cost_estimate=pl.CostEstimate(flops=flops, bytes_accessed=moved, transcendentals=0),
    )(*scalars, *args)


def struct(shape, dtype=BF):
    return jax.ShapeDtypeStruct(shape, dtype)


def iota(shape, dim):
    return lax.broadcasted_iota(jnp.int32, shape, dim)


def dot(a, b):
    return jnp.dot(a, b, preferred_element_type=F32)


def rms_norm(rows, gain):
    values = rows.astype(F32)
    scale = lax.rsqrt(jnp.mean(values * values, axis=-1, keepdims=True) + EPS)
    return (values * scale * gain).astype(BF)


def dispatch_kernel(got, tokens_out, slots_out, mix_out):
    token, row = iota((ROWS, 4 * TP), 0), iota((ROWS, 4 * TP), 1)
    pick = (token == 3 * (row >> 2) + (row & 3)) & ((row & 3) < 3)
    tokens = dot(pick.astype(F32).astype(BF), got[...]).astype(BF)
    tokens_out[...] = tokens
    meta = jnp.transpose(tokens[:, 384:512].astype(F32), (1, 0))
    first, second = meta[64:65, :], meta[65:66, :]
    expert = iota((EP, ROWS), 0).astype(F32)
    hot_a = (expert == first).astype(F32)
    hot_b = (expert == second).astype(F32)
    earlier = (iota((ROWS, ROWS), 0) < iota((ROWS, ROWS), 1)).astype(F32).astype(BF)
    count = dot((hot_a + hot_b).astype(BF), earlier)
    slot_a = first * LAND + jnp.sum(hot_a * count, axis=0, keepdims=True)
    slot_b = second * LAND + jnp.sum(hot_b * count, axis=0, keepdims=True)
    slot = iota((EP * LAND, ROWS), 0).astype(F32)
    at_a, at_b = (slot == slot_a).astype(F32), (slot == slot_b).astype(F32)
    slots_out[...] = dot((at_a + at_b).astype(BF), tokens).astype(BF)
    mix = (at_a * meta[66:67, :] + at_b * meta[67:68, :]) * (1.0 / 256.0)
    mix_out[...] = jnp.transpose(mix, (1, 0)).astype(BF)


def assemble_kernel(me, part0, part1, part2, part3, gate_out, up_out):
    for out in (gate_out, up_out):
        for half in range(2):
            out[512 * half + HALF : 512 * (half + 1), :] = jnp.zeros((64, HID), BF)
    for k, part in enumerate((part0, part1, part2, part3)):
        source = me[0] ^ k
        start = pl.multiple_of((source >> 1) * 512 + (source & 1) * FEAT, 16)
        gate_out[pl.ds(start, FEAT), :] = part[0:FEAT, :]
        up_out[pl.ds(start, FEAT), :] = part[FEAT : 2 * FEAT, :]


def dense_up_kernel(column, mate, rows, weights, out, held):
    lane = iota((BLOCK, 128), 1)

    def put(branch, first, half, width, values):
        for low, high, place in ((0, 256, 256 * branch), (256, SHARE, 512 + 64 * branch)):
            begin, end = max(first, low), min(first + BLOCK, high)
            if begin < end:
                held[place + begin - low : place + end - low, half : half + width] = values[
                    begin - first : end - first, :
                ]

    for half in range(2):
        for q in range(2):
            part = weights.at[(2 * half + q) ^ column[0]]
            tail = part[:, 768:896].astype(F32)
            tails = (tail, pltpu.roll(tail, 64, 1))
            for branch in range(2):
                put(branch, q * BLOCK, 512 * half, 384, part[:, 384 * branch : 384 * (branch + 1)])
                last = jnp.where(lane < 64, tails[branch], 0.0).astype(BF)
                put(branch, q * BLOCK, 512 * half + 384, 128, last)
    for i in range(MATES):
        out[ROWS * i : ROWS * (i + 1), :] = lax.dot_general(
            rows[mate[0] ^ i], held[...], (((1,), (1,)), ((), ())), preferred_element_type=F32
        ).astype(BF)


def expert_up_kernel(got, gate, up, dense, out):
    row, column = iota((EP * SLOT, EP * LAND), 0), iota((EP * SLOT, EP * LAND), 1)
    group = ((row.astype(F32) + 0.5) * (1.0 / SLOT)).astype(jnp.int32)
    place = row - SLOT * group
    pick = (column == LAND * group + place) & (place < CAP)
    rows = dot(pick.astype(F32).astype(BF), got[...]).astype(BF)
    for branch, weights in enumerate((gate, up)):
        pre = dot(rows, weights[...])
        other = dense[...].astype(F32)
        for z in range(Z):
            out[z, :, HID * branch : HID * (branch + 1)] = jnp.concatenate(
                [
                    pre[MOE_Z * z : MOE_Z * (z + 1)],
                    other[DENSE_Z * (2 * z + branch) : DENSE_Z * (2 * z + branch + 1)],
                ],
                axis=0,
            ).astype(BF)


def swish(gate, up):
    return gate / (1.0 + jnp.exp(-gate)) * up


def hidden_kernel(me, got, out):
    total = got[0].astype(F32)
    for z in range(1, Z):
        total = total + got[z].astype(F32)
    expert = swish(total[:MOE_Z, :HID], total[:MOE_Z, HID:])
    twice = iota((MOE_Z, HID), 1) < YH * HID - EFF
    expert = jnp.where(twice & (me[0] == YH - 1), 0.0, expert)
    pieces, tails = [], []
    for half in range(2):
        rows = total[MOE_Z:, HID * half : HID * (half + 1)]
        pieces.append(swish(rows[:, :256], rows[:, 256:512]))
        tail = rows[:, 512:640]
        tails.append(swish(tail, pltpu.roll(tail, 64, 1)))
    lane = iota((DENSE_Z, 128), 1)
    pieces.append(jnp.where(lane < 64, tails[0], pltpu.roll(tails[1], 64, 1)))
    hidden = jnp.concatenate([expert, jnp.concatenate(pieces, axis=1)], axis=0).astype(BF)
    for z in range(Z):
        out[z] = hidden


def dense_down_kernel(column, got, dense, own_out, *outs_and_held):
    *others, held = outs_and_held
    held[...] = jnp.zeros(held.shape, BF)
    for half in range(2):
        for side in range(2):
            for q in range(2):
                values = dense.at[(2 * half + q) ^ column[0]]
                first, left = q * BLOCK, 896 + 256 * side
                for low, high, step, place in ((0, 256, 256, 0), (256, SHARE, 64, 512)):
                    begin, end = max(first, low), min(first + BLOCK, high)
                    if begin < end:
                        for i in range(2):
                            at = place + step * i
                            held[2 * half + side, i, at + begin - low : at + end - low, :] = values[
                                begin - first : end - first, left : left + FEAT
                            ]
    rows = got[...].astype(F32)
    rows = jnp.concatenate(
        [rows[ROW_Z * z + MOE_Z : ROW_Z * (z + 1)] for z in range(Z)], axis=0
    ).astype(BF)
    for target in range(YH):
        sums = [dot(rows, held[target, i]) for i in range(2)]
        for mate, out in enumerate((own_out, *others)):
            pieces = []
            for z in (2 * mate, 2 * mate + 1):
                pieces += [part[DENSE_Z * z : DENSE_Z * (z + 1)] for part in sums]
            out[target] = jnp.concatenate(pieces, axis=0).astype(out.dtype)


def expert_down_kernel(me, got, part0, part1, part2, part3, out):
    rows = got[...].astype(F32)
    rows = jnp.concatenate(
        [rows[ROW_Z * z : ROW_Z * z + MOE_Z] for z in range(Z)], axis=0
    ).astype(BF)
    for k, part in enumerate((part0, part1, part2, part3)):
        out[me[0] ^ k] = lax.dot_general(
            rows, part[...], (((1,), (1,)), ((), ())), preferred_element_type=F32
        ).astype(BF)


def result_kernel(got, slots_out):
    total = got[0].astype(F32)
    for k in range(1, YH):
        total = total + got[k].astype(F32)
    slot, row = iota((EP * LAND, EP * SLOT), 0), iota((EP * LAND, EP * SLOT), 1)
    group = ((slot.astype(F32) + 0.5) * (1.0 / LAND)).astype(jnp.int32)
    place = slot - LAND * group
    pick = (row == SLOT * group + place) & (place < CAP)
    slots_out[...] = dot(pick.astype(F32).astype(BF), total.astype(BF)).astype(BF)


def turn_pairs():
    return [
        (z * EP + i, z * EP + ((i // C + z) % (YL * X)) * C + i % C)
        for z in range(Z)
        for i in range(EP)
    ]


def spread_pairs():
    pairs = []
    for z in range(Z):
        for i in range(EP):
            x, yl, c = (i % 2) * 2 + z % 2, z // 4, z // 2 % 2
            pairs.append((z * EP + i, (i // 2) * EP + yl * X * C + x * C + c))
    turned = dict(turn_pairs())
    return [(turned[source], target) for source, target in pairs]


SWAP = [(0, 1), (1, 0)]
CROSS = [(0, 3), (1, 2), (2, 1), (3, 0)]


def to_mates(first, second, third):
    return (
        lax.ppermute(first, "c", SWAP),
        lax.ppermute(second, "yl", SWAP),
        lax.ppermute(third, ("yl", "c"), CROSS),
    )


def local(
    tokens,
    gain,
    routes,
    gate_frac,
    dense_gate,
    dense_up,
    dense_down,
    expert_gate,
    expert_up,
    expert_down,
):
    position = lax.axis_index("yh")
    me = position.astype(jnp.int32).reshape(1)

    normed = rms_norm(tokens[0], gain)
    parts = jnp.pad(normed.reshape(3, Z, 2, HALF), ((0, 0), (0, 0), (0, 0), (0, 64)))
    small = jnp.concatenate([routes[0], gate_frac[0]], axis=1).astype(BF)
    small = jnp.pad(small, ((0, 0), (HALF, 60)))
    parts = parts + jnp.stack([small, jnp.zeros_like(small)], axis=1)[:, None]
    parts = jnp.pad(parts.reshape(3, Z, WIDE).transpose(1, 0, 2), ((0, 0), (0, 1), (0, 0)))
    send = jnp.broadcast_to(parts[:, None], (Z, YH, 4, WIDE)).reshape(TP, 4, WIDE)
    ups, downs = [], []
    for k in range(YH):
        start = HID * (position ^ k)
        ups.append(
            jnp.concatenate(
                [
                    lax.dynamic_slice_in_dim(expert_gate[0], start, HID, 1),
                    lax.dynamic_slice_in_dim(expert_up[0], start, HID, 1),
                ]
            )
        )
        downs.append(lax.dynamic_slice_in_dim(expert_down[0].T, start, HID, 1))

    def moved(block, k):
        return lax.ppermute(block, "yh", [(i, i ^ k) for i in range(YH)])

    for k in (1, 3):
        ups[k] = moved(ups[k], k)

    def padded(block):
        return jnp.pad(block, ((0, BLOCK - 152), (0, 0)))

    plane = ("z", "yl", "x", "c")
    gate_in, up_in, low = padded(dense_gate.T), padded(dense_up.T), padded(dense_down)
    dense = [gate_in[:, :384], up_in[:, :384], gate_in[:, 384:], up_in[:, 384:]]
    for side in range(2):
        part = low[:, FEAT * side : FEAT * (side + 1)]
        dense.append(jnp.pad(part, ((0, 0), (0, 256 - FEAT))))
    dense = lax.ppermute(jnp.concatenate(dense, axis=1), plane, turn_pairs())
    dense = lax.ppermute(dense, plane, spread_pairs())
    got = lax.all_to_all(send, ("z", "yh"), 0, 0, tiled=True).reshape(4 * TP, WIDE)
    column = lax.axis_index("x").astype(jnp.int32).reshape(1)
    own, slots, mix = call(
        dispatch_kernel,
        [struct((ROWS, WIDE)), struct((EP * LAND, WIDE)), struct((ROWS, EP * LAND))],
        [got],
        flops=2 * EP * LAND * ROWS * WIDE,
    )
    own, dense = lax.optimization_barrier((own, dense))
    mates = [lax.all_gather(own, ("yl", "c"), axis=0)]
    mate = (2 * lax.axis_index("yl") + lax.axis_index("c")).astype(jnp.int32).reshape(1)
    ups[2] = moved(ups[2], 2)
    dense = jnp.stack(
        [dense]
        + [lax.ppermute(dense, "x", [(i, i ^ k) for i in range(X)]) for k in range(1, X)]
    )
    arrived = lax.all_to_all(
        slots.reshape(EP, LAND, WIDE), ("yl", "x", "c"), 0, 0, tiled=True
    ).reshape(EP * LAND, WIDE)

    gate, up = call(
        assemble_kernel, [struct((WIDE, HID)), struct((WIDE, HID))], ups, scalars=[me]
    )
    gate, up, *mates = lax.optimization_barrier((gate, up, *mates))
    dense_pre = call(
        dense_up_kernel,
        [struct((MATES * ROWS, 2 * SHARE))],
        [*mates, dense],
        scalars=[column, mate],
        scratch=[pltpu.VMEM((2 * SHARE, WIDE), BF)],
        flops=4 * MATES * ROWS * WIDE * SHARE,
    )
    pre = call(
        expert_up_kernel,
        [struct((Z, ROW_Z, 2 * HID))],
        [arrived, gate, up, dense_pre],
        flops=4 * EP * SLOT * WIDE * HID,
    )
    pre, *downs = lax.optimization_barrier((pre, *downs))
    pre = lax.all_to_all(pre, "z", 0, 0, tiled=True)
    hidden = call(hidden_kernel, [struct((Z, ROW_Z, HID))], [pre], scalars=[me])
    downs[1:] = [moved(downs[k], k) for k in range(1, YH)]
    hidden, *downs = lax.optimization_barrier((hidden, *downs))
    hidden = lax.all_to_all(hidden, "z", 0, 0, tiled=True)
    hidden = hidden.reshape(Z * ROW_Z, HID)
    own_sum, *others = call(
        dense_down_kernel,
        [struct((YH, ROWS, FEAT), F32 if i == 0 else BF) for i in range(MATES)],
        [hidden, dense],
        scalars=[column],
        scratch=[pltpu.VMEM((YH, 2, HID, FEAT), BF)],
        flops=16 * MATES * ROWS * HID * FEAT,
    )
    from_mates = to_mates(*others)
    partial = call(
        expert_down_kernel,
        [struct((YH, EP * SLOT, FEAT))],
        [hidden, *downs],
        scalars=[me],
        flops=8 * EP * SLOT * HID * FEAT,
    )
    partial = lax.all_to_all(partial, "yh", 0, 0, tiled=True)
    result = call(
        result_kernel,
        [struct((EP * LAND, FEAT))],
        [partial],
        flops=2 * EP * LAND * EP * SLOT * FEAT,
    )
    returned = lax.all_to_all(
        result.reshape(EP, LAND, FEAT), ("yl", "x", "c"), 0, 0, tiled=True
    ).reshape(EP * LAND, FEAT)

    for sent in from_mates:
        own_sum = own_sum + sent.astype(F32)
    total = lax.dynamic_index_in_dim(own_sum, position, 0, keepdims=False)
    for k in range(1, YH):
        piece = lax.dynamic_index_in_dim(own_sum, position ^ k, 0, keepdims=False)
        total = total + moved(piece.astype(BF), k).astype(F32)
    return (total + dot(mix, returned)).astype(BF)[None]


def solution(mesh):
    split = Mesh(
        np.asarray(mesh.devices).reshape(Z, YH, YL, X, C), ("z", "yh", "yl", "x", "c")
    )
    tp, ep = ("z", "yh"), ("yl", "x", "c")
    placed = (
        P(ep, tp, None),
        P(),
        P(ep, tp, None),
        P(ep, tp, None),
        P(ep, tp),
        P(ep, tp),
        P(tp, ep),
        P(ep, tp, None),
        P(ep, tp, None),
        P(ep, None, tp),
    )
    return jax.shard_map(
        local, mesh=split, in_specs=placed, out_specs=P(ep, None, tp), check_vma=False
    )
```

```python
import jax
import jax.numpy as jnp
import numpy as np
from jax import lax
from jax.experimental import pallas as pl
from jax.experimental.pallas import tpu as pltpu
from jax.sharding import Mesh, PartitionSpec as P

D = 7168
EPS = 1e-05
Z, YH, YL, X, C = 8, 4, 2, 4, 2
EP = YL * X * C
TP = Z * YH
ROWS = 96
CAP = 18
LAND = 24
SLOT = 20
EFF = 2432
HID = 640
FEAT = 224
HALF = 448
WIDE = 1024
BLOCK = 160
SHARE = 2 * BLOCK
MATES = 4
MOE_Z = EP * SLOT // Z
DENSE_Z = MATES * ROWS // Z // 2
ROW_Z = MOE_Z + DENSE_Z
BF, F32 = jnp.bfloat16, jnp.float32


def call(kernel, outs, args, scalars=(), scratch=(), flops=0):
    specs = [pl.BlockSpec(memory_space=pltpu.SMEM)] * len(scalars)
    specs += [pl.BlockSpec(memory_space=pltpu.VMEM)] * len(args)
    moved = sum(a.size * a.dtype.itemsize for a in args)
    moved += sum(o.size * o.dtype.itemsize for o in outs)
    single = len(outs) == 1
    return pl.pallas_call(
        kernel,
        out_shape=outs[0] if single else outs,
        in_specs=specs,
        out_specs=pl.BlockSpec(memory_space=pltpu.VMEM)
        if single
        else [pl.BlockSpec(memory_space=pltpu.VMEM)] * len(outs),
        scratch_shapes=list(scratch),
        compiler_params=pltpu.CompilerParams(vmem_limit_bytes=40 * 1024 * 1024),
        cost_estimate=pl.CostEstimate(flops=flops, bytes_accessed=moved, transcendentals=0),
    )(*scalars, *args)


def struct(shape, dtype=BF):
    return jax.ShapeDtypeStruct(shape, dtype)


def iota(shape, dim):
    return lax.broadcasted_iota(jnp.int32, shape, dim)


def dot(a, b):
    return jnp.dot(a, b, preferred_element_type=F32)


def rms_norm(rows, gain):
    values = rows.astype(F32)
    scale = lax.rsqrt(jnp.mean(values * values, axis=-1, keepdims=True) + EPS)
    return (values * scale * gain).astype(BF)


def dispatch_kernel(got, tokens_out, slots_out, mix_out):
    token, row = iota((ROWS, 4 * TP), 0), iota((ROWS, 4 * TP), 1)
    pick = (token == 3 * (row >> 2) + (row & 3)) & ((row & 3) < 3)
    tokens = dot(pick.astype(F32).astype(BF), got[...]).astype(BF)
    tokens_out[...] = tokens
    meta = jnp.transpose(tokens[:, 384:512].astype(F32), (1, 0))
    first, second = meta[64:65, :], meta[65:66, :]
    expert = iota((EP, ROWS), 0).astype(F32)
    hot_a = (expert == first).astype(F32)
    hot_b = (expert == second).astype(F32)
    earlier = (iota((ROWS, ROWS), 0) < iota((ROWS, ROWS), 1)).astype(F32).astype(BF)
    count = dot((hot_a + hot_b).astype(BF), earlier)
    slot_a = first * LAND + jnp.sum(hot_a * count, axis=0, keepdims=True)
    slot_b = second * LAND + jnp.sum(hot_b * count, axis=0, keepdims=True)
    slot = iota((EP * LAND, ROWS), 0).astype(F32)
    at_a, at_b = (slot == slot_a).astype(F32), (slot == slot_b).astype(F32)
    slots_out[...] = dot((at_a + at_b).astype(BF), tokens).astype(BF)
    mix = (at_a * meta[66:67, :] + at_b * meta[67:68, :]) * (1.0 / 256.0)
    mix_out[...] = jnp.transpose(mix, (1, 0)).astype(BF)


def assemble_kernel(me, part0, part1, part2, part3, gate_out, up_out):
    for out in (gate_out, up_out):
        for half in range(2):
            out[512 * half + HALF : 512 * (half + 1), :] = jnp.zeros((64, HID), BF)
    for k, part in enumerate((part0, part1, part2, part3)):
        source = me[0] ^ k
        start = pl.multiple_of((source >> 1) * 512 + (source & 1) * FEAT, 16)
        gate_out[pl.ds(start, FEAT), :] = part[0:FEAT, :]
        up_out[pl.ds(start, FEAT), :] = part[FEAT : 2 * FEAT, :]


def dense_up_kernel(column, mate, rows, weights, out, held):
    lane = iota((BLOCK, 128), 1)

    def put(branch, first, half, width, values):
        for low, high, place in ((0, 256, 256 * branch), (256, SHARE, 512 + 64 * branch)):
            begin, end = max(first, low), min(first + BLOCK, high)
            if begin < end:
                held[place + begin - low : place + end - low, half : half + width] = values[
                    begin - first : end - first, :
                ]

    for half in range(2):
        for q in range(2):
            part = weights.at[(2 * half + q) ^ column[0]]
            tail = part[:, 768:896].astype(F32)
            tails = (tail, pltpu.roll(tail, 64, 1))
            for branch in range(2):
                put(branch, q * BLOCK, 512 * half, 384, part[:, 384 * branch : 384 * (branch + 1)])
                last = jnp.where(lane < 64, tails[branch], 0.0).astype(BF)
                put(branch, q * BLOCK, 512 * half + 384, 128, last)
    for i in range(MATES):
        out[ROWS * i : ROWS * (i + 1), :] = lax.dot_general(
            rows[mate[0] ^ i], held[...], (((1,), (1,)), ((), ())), preferred_element_type=F32
        ).astype(BF)


def expert_up_kernel(got, gate, up, dense, out):
    row, column = iota((EP * SLOT, EP * LAND), 0), iota((EP * SLOT, EP * LAND), 1)
    group = ((row.astype(F32) + 0.5) * (1.0 / SLOT)).astype(jnp.int32)
    place = row - SLOT * group
    pick = (column == LAND * group + place) & (place < CAP)
    rows = dot(pick.astype(F32).astype(BF), got[...]).astype(BF)
    for branch, weights in enumerate((gate, up)):
        pre = dot(rows, weights[...])
        other = dense[...].astype(F32)
        for z in range(Z):
            out[z, :, HID * branch : HID * (branch + 1)] = jnp.concatenate(
                [
                    pre[MOE_Z * z : MOE_Z * (z + 1)],
                    other[DENSE_Z * (2 * z + branch) : DENSE_Z * (2 * z + branch + 1)],
                ],
                axis=0,
            ).astype(BF)


def swish(gate, up):
    return gate / (1.0 + jnp.exp(-gate)) * up


def hidden_kernel(me, got, out):
    total = got[0].astype(F32)
    for z in range(1, Z):
        total = total + got[z].astype(F32)
    expert = swish(total[:MOE_Z, :HID], total[:MOE_Z, HID:])
    twice = iota((MOE_Z, HID), 1) < YH * HID - EFF
    expert = jnp.where(twice & (me[0] == YH - 1), 0.0, expert)
    pieces, tails = [], []
    for half in range(2):
        rows = total[MOE_Z:, HID * half : HID * (half + 1)]
        pieces.append(swish(rows[:, :256], rows[:, 256:512]))
        tail = rows[:, 512:640]
        tails.append(swish(tail, pltpu.roll(tail, 64, 1)))
    lane = iota((DENSE_Z, 128), 1)
    pieces.append(jnp.where(lane < 64, tails[0], pltpu.roll(tails[1], 64, 1)))
    hidden = jnp.concatenate([expert, jnp.concatenate(pieces, axis=1)], axis=0).astype(BF)
    for z in range(Z):
        out[z] = hidden


def dense_down_kernel(column, got, dense, own_out, *outs_and_held):
    *others, held = outs_and_held
    held[...] = jnp.zeros(held.shape, BF)
    for half in range(2):
        for side in range(2):
            for q in range(2):
                values = dense.at[(2 * half + q) ^ column[0]]
                first, left = q * BLOCK, 896 + 256 * side
                for low, high, step, place in ((0, 256, 256, 0), (256, SHARE, 64, 512)):
                    begin, end = max(first, low), min(first + BLOCK, high)
                    if begin < end:
                        for i in range(2):
                            at = place + step * i
                            held[2 * half + side, i, at + begin - low : at + end - low, :] = values[
                                begin - first : end - first, left : left + FEAT
                            ]
    rows = got[...].astype(F32)
    rows = jnp.concatenate(
        [rows[ROW_Z * z + MOE_Z : ROW_Z * (z + 1)] for z in range(Z)], axis=0
    ).astype(BF)
    for target in range(YH):
        sums = [dot(rows, held[target, i]) for i in range(2)]
        for mate, out in enumerate((own_out, *others)):
            pieces = []
            for z in (2 * mate, 2 * mate + 1):
                pieces += [part[DENSE_Z * z : DENSE_Z * (z + 1)] for part in sums]
            out[target] = jnp.concatenate(pieces, axis=0).astype(out.dtype)


def expert_down_kernel(me, got, part0, part1, part2, part3, out):
    rows = got[...].astype(F32)
    rows = jnp.concatenate(
        [rows[ROW_Z * z : ROW_Z * z + MOE_Z] for z in range(Z)], axis=0
    ).astype(BF)
    for k, part in enumerate((part0, part1, part2, part3)):
        out[me[0] ^ k] = lax.dot_general(
            rows, part[...], (((1,), (1,)), ((), ())), preferred_element_type=F32
        ).astype(BF)


def result_kernel(got, slots_out):
    total = got[0].astype(F32)
    for k in range(1, YH):
        total = total + got[k].astype(F32)
    slot, row = iota((EP * LAND, EP * SLOT), 0), iota((EP * LAND, EP * SLOT), 1)
    group = ((slot.astype(F32) + 0.5) * (1.0 / LAND)).astype(jnp.int32)
    place = slot - LAND * group
    pick = (row == SLOT * group + place) & (place < CAP)
    slots_out[...] = dot(pick.astype(F32).astype(BF), total.astype(BF)).astype(BF)


def turn_pairs():
    return [
        (z * EP + i, z * EP + ((i // C + z) % (YL * X)) * C + i % C)
        for z in range(Z)
        for i in range(EP)
    ]


def spread_pairs():
    pairs = []
    for z in range(Z):
        for i in range(EP):
            x, yl, c = (i % 2) * 2 + z % 2, z // 4, z // 2 % 2
            pairs.append((z * EP + i, (i // 2) * EP + yl * X * C + x * C + c))
    turned = dict(turn_pairs())
    return [(turned[source], target) for source, target in pairs]


SWAP = [(0, 1), (1, 0)]
CROSS = [(0, 3), (1, 2), (2, 1), (3, 0)]


def to_mates(first, second, third):
    return (
        lax.ppermute(first, "c", SWAP),
        lax.ppermute(second, "yl", SWAP),
        lax.ppermute(third, ("yl", "c"), CROSS),
    )


def local(
    tokens,
    gain,
    routes,
    gate_frac,
    dense_gate,
    dense_up,
    dense_down,
    expert_gate,
    expert_up,
    expert_down,
):
    position = lax.axis_index("yh")
    me = position.astype(jnp.int32).reshape(1)

    normed = rms_norm(tokens[0], gain)
    parts = jnp.pad(normed.reshape(3, Z, 2, HALF), ((0, 0), (0, 0), (0, 0), (0, 64)))
    small = jnp.concatenate([routes[0], gate_frac[0]], axis=1).astype(BF)
    small = jnp.pad(small, ((0, 0), (HALF, 60)))
    parts = parts + jnp.stack([small, jnp.zeros_like(small)], axis=1)[:, None]
    parts = jnp.pad(parts.reshape(3, Z, WIDE).transpose(1, 0, 2), ((0, 0), (0, 1), (0, 0)))
    send = jnp.broadcast_to(parts[:, None], (Z, YH, 4, WIDE)).reshape(TP, 4, WIDE)
    ups, downs = [], []
    for k in range(YH):
        start = HID * (position ^ k)
        ups.append(
            jnp.concatenate(
                [
                    lax.dynamic_slice_in_dim(expert_gate[0], start, HID, 1),
                    lax.dynamic_slice_in_dim(expert_up[0], start, HID, 1),
                ]
            )
        )
        downs.append(lax.dynamic_slice_in_dim(expert_down[0].T, start, HID, 1))

    def moved(block, k):
        return lax.ppermute(block, "yh", [(i, i ^ k) for i in range(YH)])

    for k in (1, 3):
        ups[k] = moved(ups[k], k)

    def padded(block):
        return jnp.pad(block, ((0, BLOCK - 152), (0, 0)))

    plane = ("z", "yl", "x", "c")
    gate_in, up_in, low = padded(dense_gate.T), padded(dense_up.T), padded(dense_down)
    dense = [gate_in[:, :384], up_in[:, :384], gate_in[:, 384:], up_in[:, 384:]]
    for side in range(2):
        part = low[:, FEAT * side : FEAT * (side + 1)]
        dense.append(jnp.pad(part, ((0, 0), (0, 256 - FEAT))))
    dense = lax.ppermute(jnp.concatenate(dense, axis=1), plane, turn_pairs())
    dense = lax.ppermute(dense, plane, spread_pairs())
    got = lax.all_to_all(send, ("z", "yh"), 0, 0, tiled=True).reshape(4 * TP, WIDE)
    column = lax.axis_index("x").astype(jnp.int32).reshape(1)
    own, slots, mix = call(
        dispatch_kernel,
        [struct((ROWS, WIDE)), struct((EP * LAND, WIDE)), struct((ROWS, EP * LAND))],
        [got],
        flops=2 * EP * LAND * ROWS * WIDE,
    )
    own, dense = lax.optimization_barrier((own, dense))
    mates = [lax.all_gather(own, ("yl", "c"), axis=0)]
    mate = (2 * lax.axis_index("yl") + lax.axis_index("c")).astype(jnp.int32).reshape(1)
    ups[2] = moved(ups[2], 2)
    dense = jnp.stack(
        [dense]
        + [lax.ppermute(dense, "x", [(i, i ^ k) for i in range(X)]) for k in range(1, X)]
    )
    arrived = lax.all_to_all(
        slots.reshape(EP, LAND, WIDE), ("yl", "x", "c"), 0, 0, tiled=True
    ).reshape(EP * LAND, WIDE)

    gate, up = call(
        assemble_kernel, [struct((WIDE, HID)), struct((WIDE, HID))], ups, scalars=[me]
    )
    gate, up, *mates = lax.optimization_barrier((gate, up, *mates))
    dense_pre = call(
        dense_up_kernel,
        [struct((MATES * ROWS, 2 * SHARE))],
        [*mates, dense],
        scalars=[column, mate],
        scratch=[pltpu.VMEM((2 * SHARE, WIDE), BF)],
        flops=4 * MATES * ROWS * WIDE * SHARE,
    )
    pre = call(
        expert_up_kernel,
        [struct((Z, ROW_Z, 2 * HID))],
        [arrived, gate, up, dense_pre],
        flops=4 * EP * SLOT * WIDE * HID,
    )
    pre, *downs = lax.optimization_barrier((pre, *downs))
    pre = lax.all_to_all(pre, "z", 0, 0, tiled=True)
    hidden = call(hidden_kernel, [struct((Z, ROW_Z, HID))], [pre], scalars=[me])
    downs[1:] = [moved(downs[k], k) for k in range(1, YH)]
    hidden, downs[2] = lax.optimization_barrier((hidden, downs[2]))
    hidden = lax.all_to_all(hidden, "z", 0, 0, tiled=True)
    hidden = hidden.reshape(Z * ROW_Z, HID)
    own_sum, *others = call(
        dense_down_kernel,
        [struct((YH, ROWS, FEAT), F32 if i == 0 else BF) for i in range(MATES)],
        [hidden, dense],
        scalars=[column],
        scratch=[pltpu.VMEM((YH, 2, HID, FEAT), BF)],
        flops=16 * MATES * ROWS * HID * FEAT,
    )
    from_mates = to_mates(*others)
    partial = call(
        expert_down_kernel,
        [struct((YH, EP * SLOT, FEAT))],
        [hidden, *downs],
        scalars=[me],
        flops=8 * EP * SLOT * HID * FEAT,
    )
    partial = lax.all_to_all(partial, "yh", 0, 0, tiled=True)
    result = call(
        result_kernel,
        [struct((EP * LAND, FEAT))],
        [partial],
        flops=2 * EP * LAND * EP * SLOT * FEAT,
    )
    returned = lax.all_to_all(
        result.reshape(EP, LAND, FEAT), ("yl", "x", "c"), 0, 0, tiled=True
    ).reshape(EP * LAND, FEAT)

    for sent in from_mates:
        own_sum = own_sum + sent.astype(F32)
    total = lax.dynamic_index_in_dim(own_sum, position, 0, keepdims=False)
    for k in range(1, YH):
        piece = lax.dynamic_index_in_dim(own_sum, position ^ k, 0, keepdims=False)
        total = total + moved(piece.astype(BF), k).astype(F32)
    return (total + dot(mix, returned)).astype(BF)[None]


def solution(mesh):
    split = Mesh(
        np.asarray(mesh.devices).reshape(Z, YH, YL, X, C), ("z", "yh", "yl", "x", "c")
    )
    tp, ep = ("z", "yh"), ("yl", "x", "c")
    placed = (
        P(ep, tp, None),
        P(),
        P(ep, tp, None),
        P(ep, tp, None),
        P(ep, tp),
        P(ep, tp),
        P(tp, ep),
        P(ep, tp, None),
        P(ep, tp, None),
        P(ep, None, tp),
    )
    return jax.shard_map(
        local, mesh=split, in_specs=placed, out_specs=P(ep, None, tp), check_vma=False
    )
```
